256 devices in a mesh: rep: 32 (over y, x, core), cache: 8 (over z).
Axes of the slice: x: 4, y: 4, z: 8, core: 2. Of those that a mesh axis runs over, the one named last changes fastest.
Arguments:
- queries: bfloat16 [1024, 2, 36864], P(('rep', 'cache')), may hold values from -8 to 8
- pool: bfloat16 [64, 36864], P('cache'), may hold values from -6 to 6
- prefix_pages: int32 [32, 16], P('rep'), may hold values from 0 to 63, as said below
- private_cache: bfloat16 [1024, 73728], P(('rep', 'cache')), may hold values from -6 to 6
- private_lengths: int32 [256, 4], P(('rep', 'cache')), may hold values from 1 to 128, 384 in all within a row
- hidden: bfloat16 [2048, 3584], P(('rep', 'cache')), may hold values from -6 to 6
- route_ids: int32 [2048, 8], P('rep'), may hold values from 0 to 127, all different within a row; in each aligned block of 64 rows (0 to 63, 64 to 127, ...) at most 8 rows name the same one
- route_weights: float32 [2048, 8], P('rep'), may hold values from 0.1 to 1
- w_gate: bfloat16 [128, 3584, 1024], P('rep', None, 'cache'), may hold values from -0.09375 to 0.09375
- w_up: bfloat16 [128, 3584, 1024], P('rep', None, 'cache'), may hold values from -0.09375 to 0.09375
- w_down: bfloat16 [128, 1024, 3584], P('rep', 'cache'), may hold values from -0.1875 to 0.1875
Outputs:
- attended: bfloat16 [1024, 2, 32768], P(('rep', 'cache'))
- mixed: bfloat16 [2048, 3584], P(('rep', 'cache'))
The draws below stay inside these ranges and needn't reach their ends.
Inputs may be any that keep to these rules, and one draw needn't show every extreme that they name: `prefix_pages`: each row lists 16 different pool pages; at most 4 of one row lie among the 8 pages p with the same p // 8, and in every row some such group holds exactly 4. `private_lengths`: among each device's 4 rows one has length 128. `route_ids`: A token's 8 experts differ. In each aligned block of 64 tokens (one replica's) no expert is named more than 8 times, a bound that some block reaches.
All inputs are finite; a program needn't handle non-finite values.
Results may differ from the reference program's by a relative error of at most 0.029.
Values may be sent and summed in bfloat16 or wider, within the bound.
No kernel may reach another device: no remote copies, remote signals or barrier semaphores. Data moves between devices by JAX's collectives and lax.ppermute only.
A program may use at most 128 MiB of HBM per device.

```python
import math
import jax
import jax.numpy as jnp
import numpy as np
from jax import lax

ROW_DEV = 4
HEADS = 64
LAT = 576
VAL = 512
PAGE = 64
PAGES_DEV = 8
PRIV = 128
D = 3584
FF = 1024
TOP = 8
RROWS = 32
ROWS = 1024
REP_TOK = 64
TOKENS = 2048
EXPERTS = 128
POOL_PAGES = 64
PREF_PAGES = 16
PMAX = 4
CAP = 8


def draw_pool(key, part):
    key = jax.random.fold_in(key, 5)
    latent = jnp.clip(jax.random.normal(key, (POOL_PAGES, PAGE, LAT), jnp.float32), -6.0, 6.0)
    return latent.reshape(POOL_PAGES, PAGE * LAT).astype(jnp.bfloat16)


def draw_queries(key, part):
    key = jax.random.fold_in(key, 7)
    base = jnp.clip(jax.random.normal(key, (ROWS, 2, HEADS, LAT), jnp.float32), -6.0, 6.0)
    return base.reshape(ROWS, 2, HEADS * LAT).astype(jnp.bfloat16)


def draw_prefix_pages(key, part):
    key = jax.random.fold_in(key, 3)
    owners = POOL_PAGES // PAGES_DEV
    replicas = ROWS // RROWS
    others = PREF_PAGES - PMAX
    base_count = others // (owners - 1)
    extra = others % (owners - 1)

    def one_replica(sub_key):
        hot_key, page_key, order_key = jax.random.split(sub_key, 3)
        hot_owner = jax.random.randint(hot_key, (), 0, owners)
        owner_index = jnp.arange(owners)
        offset = (owner_index - hot_owner - 1) % owners
        counts = jnp.where(owner_index == hot_owner, PMAX, base_count + (offset < extra).astype(jnp.int32))
        picks = jax.vmap(lambda page_seed: jax.random.permutation(page_seed, PAGES_DEV))(jax.random.split(page_key, owners))
        ends = jnp.cumsum(counts)
        starts = ends - counts
        entry = jnp.arange(PREF_PAGES)
        holder = jnp.sum((entry[:, None] >= ends[None, :]).astype(jnp.int32), axis=1)
        within = entry - starts[holder]
        pages = holder * PAGES_DEV + picks[holder, within]
        return jax.random.permutation(order_key, pages)
    return jax.vmap(one_replica)(jax.random.split(key, replicas)).astype(jnp.int32)


def block_scale(own_key, dims, pieces, least, high):
    level = 1.0
    for dim, parts in pieces:
        heights = jax.random.uniform(jax.random.fold_in(jax.random.fold_in(own_key, 6), dim), (parts,), jnp.float32, least / len(pieces), high / len(pieces))
        level = level * jnp.repeat(jnp.exp(heights), dims[dim] // parts).reshape((-1,) + (1,) * (len(dims) - 1 - dim))
    return level


def split_up(count, total, bound, skew):
    loads = [(1 << 20) // math.isqrt(grade ** skew) + 1 for grade in range(2, count + 1)]
    rest, given = total - bound - (count - 1), [1] * (count - 1)
    while rest > 0:
        candidates = [i for i in range(count - 1) if given[i] < bound]
        mass, budget = sum([loads[i] for i in candidates]), rest
        for i in candidates:
            more = min(bound - given[i], max(1, budget * loads[i] // mass), rest)
            given[i] = given[i] + more
            rest = rest - more
    return np.array([bound] + given)


def uneven_parts(own_key, amount, total, reach, skew):
    if amount == 2:
        one = jax.random.randint(own_key, (), max(1, total - reach), min(reach, total - 1) + 1)
        return jnp.stack([one, total - one])
    tallies = jnp.asarray(split_up(amount, total, reach, skew), jnp.int32)
    couples = (amount - 1) // 2
    source_of, sink = tallies[1:1 + 2 * couples:2], tallies[2:2 + 2 * couples:2]
    room = jnp.minimum(source_of - 1, reach - sink)
    shifted = jax.random.randint(jax.random.fold_in(own_key, 1), (couples,), 0, 1 << 20) % (room + 1)
    tallies = tallies.at[1:1 + 2 * couples:2].set(source_of - shifted).at[2:2 + 2 * couples:2].set(sink + shifted)
    return tallies[jax.random.permutation(jax.random.fold_in(own_key, 2), amount)]


def routed_block(own_key, own, number, rows, count, top, limit, lean):
    ranking = jax.random.permutation(own_key, count)
    packed, ordinary = load_shares(count, rows * top, limit, lean, True), load_shares(count, rows * top, limit, lean, False)
    places = jnp.arange(count)

    def named(lengths, offset_by):
        used = int((lengths > 0).sum())
        fixed = max(1, used // 4)
        shifted = fixed + (places - fixed + offset_by * (used - fixed)) % max(1, count - fixed)
        return jnp.zeros((count,), jnp.int32).at[ranking[jnp.where(places < fixed, places, shifted)]].set(jnp.asarray(lengths, jnp.int32))

    lengths = jnp.where(number % 4 == 0, named(packed, number // 4), named(ordinary, number - number // 4 - 1))
    mixed = jax.random.permutation(jax.random.fold_in(own, 3), count)
    donor, receiver = mixed[0:count // 2 * 2:2], mixed[1:count // 2 * 2:2]
    margin = jnp.minimum(lengths[donor] - 1, limit - lengths[receiver]) // 2
    margin = jnp.where((donor == ranking[0]) | (receiver == ranking[0]) | (lengths[receiver] == 0), 0, jnp.maximum(margin, 0))
    shifted = jax.random.randint(jax.random.fold_in(own, 4), (count // 2,), 0, 1 << 20) % (margin + 1)
    lengths = lengths.at[donor].add(-shifted).at[receiver].add(shifted)
    labels = jnp.searchsorted(jnp.cumsum(lengths), jnp.arange(rows * top), side="right").astype(jnp.int32)
    table = labels.reshape(top, rows).T
    table = table[jax.random.permutation(jax.random.fold_in(own, 1), rows)]
    offset_by = jax.random.randint(jax.random.fold_in(own, 2), (rows, 1), 0, top)
    return jnp.take_along_axis(table, (jnp.arange(top)[None, :] + offset_by) % top, axis=1)


def load_shares(amount, total, bound, skew, full):
    loads = [(1 << 20) // math.isqrt(standing ** skew) + 1 for standing in range(1, amount + 1)]
    largest = bound if full else min(bound, max(-(-total // amount), total * loads[0] // sum(loads)))
    least = 1 if total - largest >= amount - 1 else 0
    holding, spare = [largest] + [least] * (amount - 1), total - largest - least * (amount - 1)
    while spare > 0:
        free = [i for i in range(1, amount) if holding[i] < largest] or [i for i in range(1, amount) if holding[i] < bound]
        whole, remaining = sum([loads[i] for i in free]), spare
        for i in free:
            more = min(bound - holding[i], max(1, remaining * loads[i] // whole), spare)
            holding[i] = holding[i] + more
            spare = spare - more
    return np.array(holding)


def bell_draw(rng, extent, spread, most, cuts=(), kind=jnp.bfloat16):
    result = spread * jax.random.normal(rng, extent, jnp.float32)
    if cuts:
        result = result * block_scale(rng, extent, cuts, -0.22, 0.18)
    return jnp.clip(result, -most, most).astype(kind)


def setup_inputs(seed: int = 0) -> dict:
    streams_of = jax.random.split(jax.random.key(seed), 12)
    queries = draw_queries(jax.random.fold_in(streams_of[11], 71), 0)
    pool = draw_pool(jax.random.fold_in(streams_of[11], 71), 0)
    prefix_pages = draw_prefix_pages(jax.random.fold_in(streams_of[11], 71), 0)
    private_cache = bell_draw(streams_of[3], (ROWS, PRIV * LAT), 1.0, 6.0, ((0, 256),))
    private_lengths = jax.vmap(lambda own: uneven_parts(own, ROW_DEV, 3 * ROW_DEV * PRIV // 4, PRIV, 1))(jax.random.split(streams_of[4], (ROWS // ROW_DEV))).reshape((ROWS // ROW_DEV, ROW_DEV)).astype(jnp.int32)
    hidden = bell_draw(streams_of[5], (TOKENS, D), 1.0, 6.0, ((0, 256),))
    route_ids_keys = jax.random.split(jax.random.fold_in(streams_of[6], 1), TOKENS // REP_TOK)
    route_ids_turns = jax.random.permutation(jax.random.fold_in(streams_of[6], 3), TOKENS // REP_TOK)
    route_ids = jax.vmap(lambda own, number: routed_block(jax.random.fold_in(streams_of[6], 2), own, number, REP_TOK, EXPERTS, TOP, CAP, 2))(route_ids_keys, route_ids_turns).reshape((TOKENS, TOP))
    route_weights = jnp.clip(0.1 + 0.9 * jax.random.uniform(streams_of[7], (TOKENS, TOP), jnp.float32) ** block_scale(streams_of[7], (TOKENS, TOP), ((0, 32),), -0.2, 0.2), 0.1, 1.0)
    w_gate = bell_draw(streams_of[8], (EXPERTS, D, FF), D ** -0.5, 0.09375, ((0, 32), (2, 8)))
    w_up = bell_draw(streams_of[9], (EXPERTS, D, FF), D ** -0.5, 0.09375, ((0, 32), (2, 8)))
    w_down = bell_draw(streams_of[10], (EXPERTS, FF, D), FF ** -0.5, 0.1875, ((0, 32), (1, 8)))
    return {"queries": queries, "pool": pool, "prefix_pages": prefix_pages, "private_cache": private_cache, "private_lengths": private_lengths, "hidden": hidden, "route_ids": route_ids, "route_weights": route_weights, "w_gate": w_gate, "w_up": w_up, "w_down": w_down}


softmax_scale = 192.0 ** -0.5


def reference(queries, pool, prefix_pages, private_cache, private_lengths, hidden, route_ids, route_weights, w_gate, w_up, w_down):
    replicas = ROWS // RROWS
    page_table = pool.reshape(POOL_PAGES, PAGE, LAT)
    query_sets = queries.reshape(replicas, RROWS, 2 * HEADS, LAT)
    private_sets = private_cache.reshape(replicas, RROWS, PRIV, LAT)
    length_sets = private_lengths.reshape(replicas, RROWS)
    position = (jnp.arange(2 * HEADS) // HEADS).astype(jnp.int32)
    slot_numbers = jnp.arange(PRIV).astype(jnp.int32)

    def attend(operands):
        query_rows, page_list, private_rows, row_lengths = operands
        prefix_keys = page_table[page_list].reshape(PREF_PAGES * PAGE, LAT)
        flat_query = query_rows.reshape(RROWS * 2 * HEADS, LAT)
        prefix_scores = jnp.dot(flat_query, prefix_keys.T, preferred_element_type=jnp.float32) * softmax_scale
        prefix_scores = prefix_scores.reshape(RROWS, 2 * HEADS, PREF_PAGES * PAGE)
        private_scores = jnp.einsum("rqd,rjd->rqj", query_rows.astype(jnp.float32), private_rows.astype(jnp.float32)) * softmax_scale
        visible = slot_numbers[None, None, :] < (row_lengths[:, None, None] - 1 + position[None, :, None])
        peak_score = jnp.maximum(jnp.max(prefix_scores, axis=-1), jnp.max(jnp.where(visible, private_scores, -jnp.inf), axis=-1))
        prefix_exp = jnp.exp(prefix_scores - peak_score[..., None])
        private_exp = jnp.where(visible, jnp.exp(private_scores - peak_score[..., None]), 0.0)
        exp_total = jnp.sum(prefix_exp, axis=-1) + jnp.sum(private_exp, axis=-1)
        prefix_weights = prefix_exp.astype(jnp.bfloat16).reshape(RROWS * 2 * HEADS, PREF_PAGES * PAGE)
        values = jnp.dot(prefix_weights, prefix_keys[:, :VAL], preferred_element_type=jnp.float32).reshape(RROWS, 2 * HEADS, VAL)
        private_weights = lax.optimization_barrier(private_exp.astype(jnp.bfloat16)).astype(jnp.float32)
        values = values + jnp.einsum("rqj,rjv->rqv", private_weights, private_rows[:, :, :VAL].astype(jnp.float32))
        return (values / exp_total[..., None]).astype(jnp.bfloat16)

    attended = lax.map(attend, (query_sets, prefix_pages, private_sets, length_sets))
    attended = attended.reshape(ROWS, 2, HEADS * VAL)

    flat_ids = route_ids.reshape(replicas, REP_TOK * TOP)
    expert_hits = (flat_ids[..., None] == jnp.arange(EXPERTS).astype(jnp.int32)).astype(jnp.int32)
    earlier = jnp.cumsum(expert_hits, axis=1) - expert_hits
    slot_rank = jnp.sum(earlier * expert_hits, axis=-1)
    slot_place = flat_ids * CAP + slot_rank
    owner_token = (jnp.arange(REP_TOK * TOP).astype(jnp.int32) // TOP)[None, :] + (jnp.arange(replicas).astype(jnp.int32) * REP_TOK)[:, None]
    replica_index = jnp.broadcast_to(jnp.arange(replicas).astype(jnp.int32)[:, None], slot_place.shape)
    token_table = jnp.zeros((replicas, EXPERTS * CAP), jnp.int32).at[replica_index, slot_place].set(owner_token)
    weight_table = jnp.zeros((replicas, EXPERTS * CAP), jnp.float32).at[replica_index, slot_place].set(route_weights.reshape(replicas, REP_TOK * TOP))

    def expert_step(running, expert):
        chosen = lax.dynamic_slice_in_dim(token_table, expert * CAP, CAP, 1).reshape(-1)
        row_scale = lax.dynamic_slice_in_dim(weight_table, expert * CAP, CAP, 1).reshape(-1)
        inputs = hidden[chosen]
        gate_sum = jnp.dot(inputs, w_gate[expert], preferred_element_type=jnp.float32)
        up_sum = jnp.dot(inputs, w_up[expert], preferred_element_type=jnp.float32)
        inner_act = (jax.nn.silu(gate_sum) * up_sum).astype(jnp.bfloat16)
        output = jnp.dot(inner_act, w_down[expert], preferred_element_type=jnp.float32)
        return running.at[chosen].add(output * row_scale[:, None]), None

    summed, _ = lax.scan(expert_step, jnp.zeros((TOKENS, D), jnp.float32), jnp.arange(EXPERTS).astype(jnp.int32))
    return attended, summed.astype(jnp.bfloat16)
```

```python
import jax
import jax.numpy as jnp
from jax import lax
from jax.sharding import PartitionSpec as P

HEADS = 64
LAT = 576
VAL = 512
PAGE = 64
PRIV = 128
PMAX = 4
SIDE = 4
EXTRA = 128

softmax_scale = 192.0 ** (-0.5)
masked_score = -1e30


def plane_pairs(phase, step):
    pairs = []
    for y in range(SIDE):
        for x in range(SIDE):
            for core in range(2):
                if (phase == 1) == (core == 0):
                    ty, tx = y, (x + step) % SIDE
                else:
                    ty, tx = (y + step) % SIDE, x
                pairs.append(((y * SIDE + x) * 2 + core, (ty * SIDE + tx) * 2 + core))
    return pairs


def move(value, phase, step):
    return lax.ppermute(value, "rep", plane_pairs(phase, step))


def swap_core(value):
    return lax.ppermute(value, "rep", [(i, i ^ 1) for i in range(2 * SIDE * SIDE)])


def move_z(value, step, size):
    return lax.ppermute(value, "cache", [(z, (z + step) % size) for z in range(size)])


def add(*terms):
    total = terms[0].astype(jnp.float32)
    for term in terms[1:]:
        total = total + term.astype(jnp.float32)
    return total.astype(jnp.bfloat16)


def attention(queries, pool, prefix_pages, private_cache, private_lengths):
    row_count = queries.shape[0]
    my_index = lax.axis_index("cache")
    pages_held = pool.shape[0]
    listed = prefix_pages[0]
    page_total = listed.shape[0]
    holder = listed // pages_held
    order = jnp.arange(page_total)
    same = (holder[:, None] == holder[None, :]) & (order[None, :] < order[:, None])
    rank = jnp.sum(same.astype(jnp.int32), axis=1)
    slot_pick = (holder == my_index)[None, :] & (rank[None, :] == jnp.arange(PMAX)[:, None])
    local_pages = jnp.sum(jnp.where(slot_pick, listed[None, :] % pages_held, 0), axis=1)
    packed = pool[local_pages]
    gathered = lax.all_gather(packed, "cache", axis=0, tiled=True)
    key_rows = gathered[holder * PMAX + rank].reshape(page_total * PAGE, LAT)

    query_rows = queries.reshape(row_count, 2 * HEADS, LAT)
    query_flat = queries.reshape(row_count * 2 * HEADS, LAT)
    private_rows = private_cache.reshape(row_count, PRIV, LAT)
    private_scores = (
        jnp.einsum("rqd,rjd->rqj", query_rows, private_rows, preferred_element_type=jnp.float32)
        * softmax_scale
    )
    position = jnp.arange(2 * HEADS) // HEADS
    visible = (
        jnp.arange(PRIV)[None, None, :]
        < private_lengths[0][:, None, None] - 1 + position[None, :, None]
    )
    private_scores = jnp.where(visible, private_scores, masked_score)
    private_peak = jnp.max(private_scores, axis=-1)
    private_exp = jnp.where(visible, jnp.exp(private_scores - private_peak[..., None]), 0.0)
    private_values = jnp.einsum(
        "rqj,rjv->rqv",
        private_exp.astype(jnp.bfloat16),
        private_rows[:, :, :VAL],
        preferred_element_type=jnp.float32,
    ).reshape(-1, VAL)
    private_peak = private_peak.reshape(-1)
    private_sum = jnp.sum(private_exp, axis=-1).reshape(-1)

    scores = (
        jnp.einsum("qd,kd->qk", query_flat, key_rows, preferred_element_type=jnp.float32)
        * softmax_scale
    )
    peak = jnp.maximum(private_peak, jnp.max(scores, axis=-1))
    weights = jnp.exp(scores - peak[:, None])
    rescale = jnp.exp(private_peak - peak)
    weight_sum = private_sum * rescale + jnp.sum(weights, axis=-1)
    value_sum = private_values * rescale[:, None] + jnp.dot(
        weights.astype(jnp.bfloat16), key_rows[:, :VAL], preferred_element_type=jnp.float32
    )
    attended = (value_sum / weight_sum[:, None]).astype(jnp.bfloat16)
    return attended.reshape(row_count, 2, HEADS * VAL)


def experts(hidden, route_ids, route_weights, w_gate, w_up, w_down):
    cache_size = lax.axis_size("cache")
    token_count, width = hidden.shape
    top_count = route_ids.shape[1]
    local_experts, _, hidden_units = w_gate.shape
    columns = local_experts * hidden_units
    start = lax.axis_index("cache") * token_count
    ids = lax.dynamic_slice_in_dim(route_ids, start, token_count, 0)
    scale = lax.dynamic_slice_in_dim(route_weights, start, token_count, 0)
    high = lax.reduce_precision(scale, 8, 7)
    low = lax.reduce_precision(scale - high, 8, 7)
    routing = jnp.concatenate(
        [
            ids.astype(jnp.bfloat16),
            high.astype(jnp.bfloat16),
            low.astype(jnp.bfloat16),
            jnp.zeros((token_count, EXTRA - 3 * top_count), jnp.bfloat16),
        ],
        axis=1,
    )
    own = jnp.concatenate([hidden, routing], axis=1)
    block = jnp.concatenate(
        [own] + [move_z(own, step, cache_size) for step in range(1, cache_size)], axis=0
    )

    both = jnp.concatenate([w_gate, w_up], axis=0)
    both = jnp.transpose(both, (1, 0, 2)).reshape(width, 2 * columns)
    both = jnp.concatenate([both, jnp.zeros((EXTRA, 2 * columns), jnp.bfloat16)], axis=0)
    down = w_down.reshape(columns, width)
    column_expert = (
        lax.axis_index("rep") * local_experts + jnp.arange(columns) // hidden_units
    ).astype(jnp.float32)

    def work(rows):
        sums = jnp.dot(rows, both, preferred_element_type=jnp.float32)
        routed = rows[:, width:].astype(jnp.float32)
        gain = 0.0
        for k in range(top_count):
            value = routed[:, top_count + k] + routed[:, 2 * top_count + k]
            hit = routed[:, k][:, None] == column_expert[None, :]
            gain = gain + jnp.where(hit, value[:, None], 0.0)
        gate, up = sums[:, :columns], sums[:, columns:]
        inner = (jax.nn.silu(gate) * up * gain).astype(jnp.bfloat16)
        return jnp.dot(inner, down, preferred_element_type=jnp.float32).astype(jnp.bfloat16)

    size = block.shape[0]
    before = move(block, 1, 1)
    after = move(block, 1, -1)
    across = jnp.concatenate(
        [move(before[: size // 2], 1, 1), move(after[size // 2 :], 1, -1)], axis=0
    )
    piece = jnp.concatenate([block, before, after, across], axis=0)
    half = piece.shape[0] // 2
    piece_before = move(piece, 2, 1)
    piece_after = move(piece, 2, -1)
    piece_across = jnp.concatenate(
        [move(piece_before[:half], 2, 1), move(piece_after[half:], 2, -1)], axis=0
    )

    def chip_sum(rows):
        theirs = work(swap_core(rows))
        return add(work(rows), swap_core(theirs))

    sum_own = chip_sum(piece)
    sum_before = chip_sum(piece_before)
    sum_after = chip_sum(piece_after)
    back_low = move(sum_before[half:], 2, -1)
    back_high = move(sum_after[:half], 2, 1)
    sum_across = chip_sum(piece_across)
    via_before = move(sum_across[:half], 2, -1)
    via_after = move(sum_across[half:], 2, 1)
    forth_high = move(add(sum_before[:half], via_before), 2, -1)
    forth_low = move(add(sum_after[half:], via_after), 2, 1)
    line_high = add(sum_own[:half], forth_high, back_high)
    line_low = add(sum_own[half:], back_low, forth_low)

    own_sum, before_sum = line_high[:size], line_high[size:]
    after_sum, across_sum = line_low[:size], line_low[size:]
    cut = size // 2
    via_before = move(across_sum[:cut], 1, -1)
    via_after = move(across_sum[cut:], 1, 1)
    back_low = move(before_sum[cut:], 1, -1)
    back_high = move(after_sum[:cut], 1, 1)
    forth_high = move(add(before_sum[:cut], via_before), 1, -1)
    forth_low = move(add(after_sum[cut:], via_after), 1, 1)
    replica = jnp.concatenate(
        [
            add(own_sum[:cut], forth_high, back_high),
            add(own_sum[cut:], back_low, forth_low),
        ],
        axis=0,
    )
    parts = replica.reshape(cache_size, token_count, width)
    return add(
        parts[0], *[move_z(parts[step], -step, cache_size) for step in range(1, cache_size)]
    )


def per_device(
    queries,
    pool,
    prefix_pages,
    private_cache,
    private_lengths,
    hidden,
    route_ids,
    route_weights,
    w_gate,
    w_up,
    w_down,
):
    attended = attention(queries, pool, prefix_pages, private_cache, private_lengths)
    mixed = experts(hidden, route_ids, route_weights, w_gate, w_up, w_down)
    return (attended, mixed)


def solution(mesh):
    in_specs = (
        P(("rep", "cache"), None, None),
        P("cache", None),
        P("rep", None),
        P(("rep", "cache"), None),
        P(("rep", "cache"), None),
        P(("rep", "cache"), None),
        P("rep", None),
        P("rep", None),
        P("rep", None, "cache"),
        P("rep", None, "cache"),
        P("rep", "cache", None),
    )
    out_specs = (P(("rep", "cache"), None, None), P(("rep", "cache"), None))
    return jax.shard_map(
        per_device, mesh=mesh, in_specs=in_specs, out_specs=out_specs, check_vma=False
    )
```

```python
import functools

import jax
import jax.numpy as jnp
from jax import lax
from jax.experimental import pallas as pl
from jax.experimental.pallas import tpu as pltpu
from jax.sharding import PartitionSpec as P

HEADS = 64
LAT = 576
VAL = 512
PAGE = 64
PRIV = 128
PMAX = 4
SIDE = 4
EXTRA = 128

softmax_scale = 192.0 ** (-0.5)
masked_score = -1e30


def plane_pairs(phase, step):
    pairs = []
    for y in range(SIDE):
        for x in range(SIDE):
            for core in range(2):
                if (phase == 1) == (core == 0):
                    ty, tx = y, (x + step) % SIDE
                else:
                    ty, tx = (y + step) % SIDE, x
                pairs.append(((y * SIDE + x) * 2 + core, (ty * SIDE + tx) * 2 + core))
    return pairs


def move(value, phase, step):
    return lax.ppermute(value, "rep", plane_pairs(phase, step))


def swap_core(value):
    return lax.ppermute(value, "rep", [(i, i ^ 1) for i in range(2 * SIDE * SIDE)])


def after_all(*values):
    return lax.optimization_barrier(values)


def move_z(value, step, size):
    return lax.ppermute(value, "cache", [(z, (z + step) % size) for z in range(size)])


VMEM_BYTES = 48 * 1024 * 1024
SMALL = pl.CostEstimate(flops=1, bytes_accessed=1, transcendentals=0)
whole = pl.BlockSpec(memory_space=pltpu.VMEM)


def pack_kernel(*refs):
    *parts, out = refs
    rows = parts[0].shape[0]
    if rows % 16 == 0:
        for i, part in enumerate(parts):
            out[i * rows : (i + 1) * rows] = part[...]
    else:
        for i in range(0, len(parts), 2):
            pair = [parts[i + k][...].astype(jnp.float32) for k in range(2)]
            out[i * rows : (i + 2) * rows] = jnp.concatenate(pair, axis=0).astype(out.dtype)


def pack(parts):
    rows, width = parts[0].shape
    return pl.pallas_call(
        pack_kernel,
        out_shape=jax.ShapeDtypeStruct((rows * len(parts), width), parts[0].dtype),
        in_specs=[whole] * len(parts),
        out_specs=whole,
        compiler_params=pltpu.CompilerParams(vmem_limit_bytes=VMEM_BYTES),
        cost_estimate=SMALL,
    )(*parts)


def halves_kernel(first, second, low, high):
    low[...] = first[...]
    high[...] = second[...]


def halves(first, second):
    rows, width = first.shape
    part = jax.ShapeDtypeStruct((rows // 2, width), first.dtype)
    return pl.pallas_call(
        halves_kernel,
        grid=(1,),
        out_shape=[part] * 2,
        in_specs=[
            pl.BlockSpec((rows // 2, width), lambda j: (0, j)),
            pl.BlockSpec((rows // 2, width), lambda j: (1, j)),
        ],
        out_specs=[pl.BlockSpec((rows // 2, width), lambda j: (0, j))] * 2,
        compiler_params=pltpu.CompilerParams(vmem_limit_bytes=VMEM_BYTES),
        cost_estimate=SMALL,
    )(first, second)


def sum_kernel(term_count, *refs):
    terms, outs = refs[:term_count], refs[term_count:]
    total = terms[0][...].astype(jnp.float32)
    for term in terms[1:]:
        total = total + term[...].astype(jnp.float32)
    rows = outs[0].shape[0]
    for i, out in enumerate(outs):
        out[...] = total[i * rows : (i + 1) * rows].astype(out.dtype)


def sum_split(terms, split):
    rows, width = terms[0].shape
    tile = 896
    part = jax.ShapeDtypeStruct((rows // split, width), terms[0].dtype)
    return pl.pallas_call(
        functools.partial(sum_kernel, len(terms)),
        grid=(width // tile,),
        out_shape=[part] * split,
        in_specs=[pl.BlockSpec((rows, tile), lambda j: (0, j))] * len(terms),
        out_specs=[pl.BlockSpec((rows // split, tile), lambda j: (0, j))] * split,
        compiler_params=pltpu.CompilerParams(vmem_limit_bytes=VMEM_BYTES),
        cost_estimate=SMALL,
    )(*terms)


def expert_kernel(groups, adds, top_count, first, *refs):
    count = sum(groups)
    rows, plus = refs[:count], refs[count : count + adds]
    w_gate, w_up, w_down = refs[count + adds : count + adds + 3]
    outs = refs[count + adds + 3 : count + adds + 3 + len(groups)]
    both, down, inner, tokens, arrived = refs[count + adds + 3 + len(groups) :]
    local, width, units = w_gate.shape
    fetches = []
    for expert in range(local):
        for k, weight in enumerate((w_gate, w_up)):
            fetches.append(
                pltpu.make_async_copy(
                    weight.at[expert],
                    both.at[expert, :, k * units : (k + 1) * units],
                    arrived.at[2 * expert + k],
                )
            )
    fetches.append(pltpu.make_async_copy(w_down, down, arrived.at[2 * local]))
    for fetch in fetches:
        fetch.start()
    sources = []
    for group in groups:
        parts, rows = rows[:group], rows[group:]
        if group == 1:
            sources.append(parts[0])
        else:
            size = parts[0].shape[0]
            for i, part in enumerate(parts):
                tokens[len(sources), i * size : (i + 1) * size] = part[...]
            sources.append(tokens.at[len(sources)])
    for expert in range(local):
        fetches[2 * expert].wait()
        fetches[2 * expert + 1].wait()
        name = (first[0] + expert).astype(jnp.float32)
        for i, x in enumerate(sources):
            sums = jnp.dot(x[:, :width], both[expert], preferred_element_type=jnp.float32)
            gate, up = sums[:, :units], sums[:, units:]
            routed = x[:, width:].astype(jnp.float32)
            lane = lax.broadcasted_iota(jnp.int32, routed.shape, 1)
            value = pltpu.roll(routed, EXTRA - top_count, 1) + pltpu.roll(
                routed, EXTRA - 2 * top_count, 1
            )
            hit = (routed == name) & (lane < top_count)
            gain = jnp.sum(jnp.where(hit, value, 0.0), axis=1, keepdims=True)
            act = gate / (1.0 + jnp.exp(-gate)) * up * gain
            inner[i, :, expert * units : (expert + 1) * units] = act.astype(inner.dtype)
    fetches[2 * local].wait()
    step = 896
    for i, out in enumerate(outs):
        for j in range(0, width, step):
            part = jnp.dot(inner[i], down[:, j : j + step], preferred_element_type=jnp.float32)
            if adds:
                part = part + plus[i][:, j : j + step].astype(jnp.float32)
            out[:, j : j + step] = part.astype(out.dtype)


def run_experts(pieces, plus, first, w_gate, w_up, w_down, top_count):
    local, width, units = w_gate.shape
    columns = local * units
    groups = [len(piece) for piece in pieces]
    rows = [part for piece in pieces for part in piece]
    size = sum(part.shape[0] for part in pieces[0])
    split = any(group > 1 for group in groups)
    return pl.pallas_call(
        functools.partial(expert_kernel, groups, len(plus), top_count),
        out_shape=[jax.ShapeDtypeStruct((size, width), jnp.bfloat16)] * len(pieces),
        in_specs=[pl.BlockSpec(memory_space=pltpu.SMEM)]
        + [whole] * (len(rows) + len(plus))
        + [pl.BlockSpec(memory_space=pl.ANY)] * 3,
        out_specs=[whole] * len(pieces),
        scratch_shapes=[
            pltpu.VMEM((local, width, 2 * units), jnp.bfloat16),
            pltpu.VMEM((columns, width), jnp.bfloat16),
            pltpu.VMEM((len(pieces), size, columns), jnp.bfloat16),
            pltpu.VMEM((len(pieces), size if split else 16, width + EXTRA), jnp.bfloat16),
            pltpu.SemaphoreType.DMA((2 * local + 1,)),
        ],
        compiler_params=pltpu.CompilerParams(vmem_limit_bytes=VMEM_BYTES),
        cost_estimate=SMALL,
    )(first, *rows, *plus, w_gate, w_up, w_down.reshape(columns, width))


def held_pages(pool, prefix_pages):
    my_index = lax.axis_index("cache")
    pages_held = pool.shape[0]
    listed = prefix_pages[0]
    page_total = listed.shape[0]
    holder = listed // pages_held
    order = jnp.arange(page_total)
    same = (holder[:, None] == holder[None, :]) & (order[None, :] < order[:, None])
    rank = jnp.sum(same.astype(jnp.int32), axis=1)
    slot_pick = (holder == my_index)[None, :] & (rank[None, :] == jnp.arange(PMAX)[:, None])
    local_pages = jnp.sum(jnp.where(slot_pick, listed[None, :] % pages_held, 0), axis=1)
    return pool[local_pages], (holder, rank)


def private_attention(queries, private_cache, private_lengths):
    row_count = queries.shape[0]
    query_rows = queries.reshape(row_count, 2 * HEADS, LAT)
    private_rows = private_cache.reshape(row_count, PRIV, LAT)
    private_scores = (
        jnp.einsum("rqd,rjd->rqj", query_rows, private_rows, preferred_element_type=jnp.float32)
        * softmax_scale
    )
    position = jnp.arange(2 * HEADS) // HEADS
    visible = (
        jnp.arange(PRIV)[None, None, :]
        < private_lengths[0][:, None, None] - 1 + position[None, :, None]
    )
    private_scores = jnp.where(visible, private_scores, masked_score)
    private_peak = jnp.max(private_scores, axis=-1)
    private_exp = jnp.where(visible, jnp.exp(private_scores - private_peak[..., None]), 0.0)
    private_values = jnp.einsum(
        "rqj,rjv->rqv",
        private_exp.astype(jnp.bfloat16),
        private_rows[:, :, :VAL],
        preferred_element_type=jnp.float32,
    ).reshape(-1, VAL)
    query_flat = query_rows.reshape(row_count * 2 * HEADS, LAT)
    return query_flat, private_peak.reshape(-1), jnp.sum(private_exp, axis=-1).reshape(-1), private_values


def finish_attention(private, gathered, places, row_count):
    query_flat, private_peak, private_sum, private_values = private
    key_rows = gathered[places].reshape(places[0].shape[0] * PAGE, LAT)
    scores = (
        jnp.einsum("qd,kd->qk", query_flat, key_rows, preferred_element_type=jnp.float32)
        * softmax_scale
    )
    peak = jnp.maximum(private_peak, jnp.max(scores, axis=-1))
    weights = jnp.exp(scores - peak[:, None])
    rescale = jnp.exp(private_peak - peak)
    weight_sum = private_sum * rescale + jnp.sum(weights, axis=-1)
    value_sum = private_values * rescale[:, None] + jnp.dot(
        weights.astype(jnp.bfloat16), key_rows[:, :VAL], preferred_element_type=jnp.float32
    )
    attended = (value_sum / weight_sum[:, None]).astype(jnp.bfloat16)
    return attended.reshape(row_count, 2, HEADS * VAL)


def experts(packed, late, hidden, route_ids, route_weights, w_gate, w_up, w_down):
    cache_size = lax.axis_size("cache")
    token_count, width = hidden.shape
    top_count = route_ids.shape[1]
    local_experts = w_gate.shape[0]
    start = lax.axis_index("cache") * token_count
    ids = lax.dynamic_slice_in_dim(route_ids, start, token_count, 0)
    scale = lax.dynamic_slice_in_dim(route_weights, start, token_count, 0)
    high = lax.reduce_precision(scale, 8, 7)
    low = lax.reduce_precision(scale - high, 8, 7)
    routing = jnp.concatenate(
        [
            ids.astype(jnp.bfloat16),
            high.astype(jnp.bfloat16),
            low.astype(jnp.bfloat16),
            jnp.zeros((token_count, EXTRA - 3 * top_count), jnp.bfloat16),
        ],
        axis=1,
    )
    own = jnp.concatenate([hidden, routing], axis=1)
    own, packed = after_all(own, packed)
    gathered = lax.all_gather(packed, "cache", axis=0, tiled=False)
    block = pack([own] + [move_z(own, step, cache_size) for step in range(1, cache_size)])
    first = (lax.axis_index("rep") * local_experts).astype(jnp.int32).reshape(1)

    def work(pieces, plus=()):
        return run_experts(pieces, plus, first, w_gate, w_up, w_down, top_count)

    piece = pack([block, move(block, 1, 1), move(block, 1, -1), move(block, 1, 2)])
    before, after = move(piece, 2, 1), move(piece, 2, -1)
    own_there, own_here = work([[swap_core(piece)], [piece]])
    own_back = swap_core(own_there)
    before, after, own_here, own_there = after_all(before, after, own_here, own_there)
    low, high = halves(before, after)
    low, high = move(low, 2, 1), move(high, 2, -1)
    side_there = work([[swap_core(before)], [swap_core(after)]])
    low, high, *side_there = after_all(low, high, *side_there)
    side_back = [swap_core(part) for part in side_there]
    across_other = [swap_core(low), swap_core(high)]
    (across_here,) = work([[low, high]])
    before, after, across_here = after_all(before, after, across_here)
    sum_before, sum_after = work([[before], [after]], side_back)
    *across_other, sum_before, sum_after = after_all(*across_other, sum_before, sum_after)
    from_after, from_before = move(sum_before, 2, -1), move(sum_after, 2, 1)
    (across_there,) = work([across_other])
    across_back = swap_core(across_there)
    (line_part,) = sum_split([own_here, own_back, from_after, from_before], 1)
    across_here, line_part = after_all(across_here, line_part)
    (sum_across,) = sum_split([across_here, across_back], 1)
    *late, sum_across = after_all(*late, sum_across)
    from_across = move(sum_across, 2, 2)
    line = sum_split([line_part, from_across], SIDE)
    parts = sum_split(
        [line[0], move(line[1], 1, -1), move(line[2], 1, 1), move(line[3], 1, 2)], cache_size
    )
    arrived = [move_z(parts[step], -step, cache_size) for step in range(1, cache_size)]
    return gathered, late, sum_split([parts[0]] + arrived, 1)[0]


def per_device(
    queries,
    pool,
    prefix_pages,
    private_cache,
    private_lengths,
    hidden,
    route_ids,
    route_weights,
    w_gate,
    w_up,
    w_down,
):
    packed, places = held_pages(pool, prefix_pages)
    late = (queries, private_cache, private_lengths, *places)
    gathered, late, mixed = experts(
        packed, late, hidden, route_ids, route_weights, w_gate, w_up, w_down
    )
    queries, private_cache, private_lengths, *places = late
    private = private_attention(queries, private_cache, private_lengths)
    attended = finish_attention(private, gathered, tuple(places), queries.shape[0])
    return (attended, mixed)


def solution(mesh):
    in_specs = (
        P(("rep", "cache"), None, None),
        P("cache", None),
        P("rep", None),
        P(("rep", "cache"), None),
        P(("rep", "cache"), None),
        P(("rep", "cache"), None),
        P("rep", None),
        P("rep", None),
        P("rep", None, "cache"),
        P("rep", None, "cache"),
        P("rep", "cache", None),
    )
    out_specs = (P(("rep", "cache"), None, None), P(("rep", "cache"), None))
    return jax.shard_map(
        per_device, mesh=mesh, in_specs=in_specs, out_specs=out_specs, check_vma=False
    )
```

```python
import functools

import jax
import jax.numpy as jnp
from jax import lax
from jax.experimental import pallas as pl
from jax.experimental.pallas import tpu as pltpu
from jax.sharding import PartitionSpec as P

HEADS = 64
LAT = 576
VAL = 512
PAGE = 64
PRIV = 128
PMAX = 4
SIDE = 4
EXTRA = 128

softmax_scale = 192.0 ** (-0.5)
masked_score = -1e30


def plane_pairs(phase, step):
    pairs = []
    for y in range(SIDE):
        for x in range(SIDE):
            for core in range(2):
                if (phase == 1) == (core == 0):
                    ty, tx = y, (x + step) % SIDE
                else:
                    ty, tx = (y + step) % SIDE, x
                pairs.append(((y * SIDE + x) * 2 + core, (ty * SIDE + tx) * 2 + core))
    return pairs


def move(value, phase, step):
    return lax.ppermute(value, "rep", plane_pairs(phase, step))


def swap_core(value):
    return lax.ppermute(value, "rep", [(i, i ^ 1) for i in range(2 * SIDE * SIDE)])


def after_all(*values):
    return lax.optimization_barrier(values)


def move_z(value, step, size):
    return lax.ppermute(value, "cache", [(z, (z + step) % size) for z in range(size)])


VMEM_BYTES = 48 * 1024 * 1024
SMALL = pl.CostEstimate(flops=1, bytes_accessed=1, transcendentals=0)
whole = pl.BlockSpec(memory_space=pltpu.VMEM)


def pack_kernel(*refs):
    *parts, out = refs
    rows = parts[0].shape[0]
    if rows % 16 == 0:
        for i, part in enumerate(parts):
            out[i * rows : (i + 1) * rows] = part[...]
    else:
        for i in range(0, len(parts), 2):
            pair = [parts[i + k][...].astype(jnp.float32) for k in range(2)]
            out[i * rows : (i + 2) * rows] = jnp.concatenate(pair, axis=0).astype(out.dtype)


def pack(parts):
    rows, width = parts[0].shape
    return pl.pallas_call(
        pack_kernel,
        out_shape=jax.ShapeDtypeStruct((rows * len(parts), width), parts[0].dtype),
        in_specs=[whole] * len(parts),
        out_specs=whole,
        compiler_params=pltpu.CompilerParams(vmem_limit_bytes=VMEM_BYTES),
        cost_estimate=SMALL,
    )(*parts)


def halves_kernel(first, second, low, high):
    low[...] = first[...]
    high[...] = second[...]


def halves(first, second):
    rows, width = first.shape
    part = jax.ShapeDtypeStruct((rows // 2, width), first.dtype)
    return pl.pallas_call(
        halves_kernel,
        grid=(1,),
        out_shape=[part] * 2,
        in_specs=[
            pl.BlockSpec((rows // 2, width), lambda j: (0, j)),
            pl.BlockSpec((rows // 2, width), lambda j: (1, j)),
        ],
        out_specs=[pl.BlockSpec((rows // 2, width), lambda j: (0, j))] * 2,
        compiler_params=pltpu.CompilerParams(vmem_limit_bytes=VMEM_BYTES),
        cost_estimate=SMALL,
    )(first, second)


def sum_kernel(term_count, *refs):
    terms, outs = refs[:term_count], refs[term_count:]
    total = terms[0][...].astype(jnp.float32)
    for term in terms[1:]:
        total = total + term[...].astype(jnp.float32)
    rows = outs[0].shape[0]
    for i, out in enumerate(outs):
        out[...] = total[i * rows : (i + 1) * rows].astype(out.dtype)


def sum_split(terms, split):
    rows, width = terms[0].shape
    tile = 896
    part = jax.ShapeDtypeStruct((rows // split, width), terms[0].dtype)
    return pl.pallas_call(
        functools.partial(sum_kernel, len(terms)),
        grid=(width // tile,),
        out_shape=[part] * split,
        in_specs=[pl.BlockSpec((rows, tile), lambda j: (0, j))] * len(terms),
        out_specs=[pl.BlockSpec((rows // split, tile), lambda j: (0, j))] * split,
        compiler_params=pltpu.CompilerParams(vmem_limit_bytes=VMEM_BYTES),
        cost_estimate=SMALL,
    )(*terms)


def expert_kernel(groups, adds, top_count, first, *refs):
    count = sum(groups)
    rows, plus = refs[:count], refs[count : count + adds]
    w_gate, w_up, w_down = refs[count + adds : count + adds + 3]
    outs = refs[count + adds + 3 : count + adds + 3 + len(groups)]
    both, down, inner, tokens, arrived = refs[count + adds + 3 + len(groups) :]
    local, width, units = w_gate.shape
    fetches = []
    for expert in range(local):
        for k, weight in enumerate((w_gate, w_up)):
            fetches.append(
                pltpu.make_async_copy(
                    weight.at[expert],
                    both.at[expert, :, k * units : (k + 1) * units],
                    arrived.at[2 * expert + k],
                )
            )
    fetches.append(pltpu.make_async_copy(w_down, down, arrived.at[2 * local]))
    for fetch in fetches:
        fetch.start()
    sources = []
    for group in groups:
        parts, rows = rows[:group], rows[group:]
        if group == 1:
            sources.append(parts[0])
        else:
            size = parts[0].shape[0]
            for i, part in enumerate(parts):
                tokens[len(sources), i * size : (i + 1) * size] = part[...]
            sources.append(tokens.at[len(sources)])
    for expert in range(local):
        fetches[2 * expert].wait()
        fetches[2 * expert + 1].wait()
        name = (first[0] + expert).astype(jnp.float32)
        for i, x in enumerate(sources):
            sums = jnp.dot(x[:, :width], both[expert], preferred_element_type=jnp.float32)
            gate, up = sums[:, :units], sums[:, units:]
            routed = x[:, width:].astype(jnp.float32)
            lane = lax.broadcasted_iota(jnp.int32, routed.shape, 1)
            value = pltpu.roll(routed, EXTRA - top_count, 1) + pltpu.roll(
                routed, EXTRA - 2 * top_count, 1
            )
            hit = (routed == name) & (lane < top_count)
            gain = jnp.sum(jnp.where(hit, value, 0.0), axis=1, keepdims=True)
            act = gate / (1.0 + jnp.exp(-gate)) * up * gain
            inner[i, :, expert * units : (expert + 1) * units] = act.astype(inner.dtype)
    fetches[2 * local].wait()
    step = 896
    for i, out in enumerate(outs):
        for j in range(0, width, step):
            part = jnp.dot(inner[i], down[:, j : j + step], preferred_element_type=jnp.float32)
            if adds:
                part = part + plus[i][:, j : j + step].astype(jnp.float32)
            out[:, j : j + step] = part.astype(out.dtype)


def run_experts(pieces, plus, first, w_gate, w_up, w_down, top_count):
    local, width, units = w_gate.shape
    columns = local * units
    groups = [len(piece) for piece in pieces]
    rows = [part for piece in pieces for part in piece]
    size = sum(part.shape[0] for part in pieces[0])
    split = any(group > 1 for group in groups)
    return pl.pallas_call(
        functools.partial(expert_kernel, groups, len(plus), top_count),
        out_shape=[jax.ShapeDtypeStruct((size, width), jnp.bfloat16)] * len(pieces),
        in_specs=[pl.BlockSpec(memory_space=pltpu.SMEM)]
        + [whole] * (len(rows) + len(plus))
        + [pl.BlockSpec(memory_space=pl.ANY)] * 3,
        out_specs=[whole] * len(pieces),
        scratch_shapes=[
            pltpu.VMEM((local, width, 2 * units), jnp.bfloat16),
            pltpu.VMEM((columns, width), jnp.bfloat16),
            pltpu.VMEM((len(pieces), size, columns), jnp.bfloat16),
            pltpu.VMEM((len(pieces), size if split else 16, width + EXTRA), jnp.bfloat16),
            pltpu.SemaphoreType.DMA((2 * local + 1,)),
        ],
        compiler_params=pltpu.CompilerParams(vmem_limit_bytes=VMEM_BYTES),
        cost_estimate=SMALL,
    )(first, *rows, *plus, w_gate, w_up, w_down.reshape(columns, width))


def held_pages(pool, prefix_pages):
    my_index = lax.axis_index("cache")
    pages_held = pool.shape[0]
    listed = prefix_pages[0]
    page_total = listed.shape[0]
    holder = listed // pages_held
    order = jnp.arange(page_total)
    same = (holder[:, None] == holder[None, :]) & (order[None, :] < order[:, None])
    rank = jnp.sum(same.astype(jnp.int32), axis=1)
    slot_pick = (holder == my_index)[None, :] & (rank[None, :] == jnp.arange(PMAX)[:, None])
    local_pages = jnp.sum(jnp.where(slot_pick, listed[None, :] % pages_held, 0), axis=1)
    return pool[local_pages], (holder, rank)


def private_attention(queries, private_cache, private_lengths):
    row_count = queries.shape[0]
    query_rows = queries.reshape(row_count, 2 * HEADS, LAT)
    private_rows = private_cache.reshape(row_count, PRIV, LAT)
    private_scores = (
        jnp.einsum("rqd,rjd->rqj", query_rows, private_rows, preferred_element_type=jnp.float32)
        * softmax_scale
    )
    position = jnp.arange(2 * HEADS) // HEADS
    visible = (
        jnp.arange(PRIV)[None, None, :]
        < private_lengths[0][:, None, None] - 1 + position[None, :, None]
    )
    private_scores = jnp.where(visible, private_scores, masked_score)
    private_peak = jnp.max(private_scores, axis=-1)
    private_exp = jnp.where(visible, jnp.exp(private_scores - private_peak[..., None]), 0.0)
    private_values = jnp.einsum(
        "rqj,rjv->rqv",
        private_exp.astype(jnp.bfloat16),
        private_rows[:, :, :VAL],
        preferred_element_type=jnp.float32,
    ).reshape(-1, VAL)
    query_flat = query_rows.reshape(row_count * 2 * HEADS, LAT)
    return query_flat, private_peak.reshape(-1), jnp.sum(private_exp, axis=-1).reshape(-1), private_values


def finish_attention(private, gathered, places, row_count):
    query_flat, private_peak, private_sum, private_values = private
    key_rows = gathered[places].reshape(places[0].shape[0] * PAGE, LAT)
    scores = (
        jnp.einsum("qd,kd->qk", query_flat, key_rows, preferred_element_type=jnp.float32)
        * softmax_scale
    )
    peak = jnp.maximum(private_peak, jnp.max(scores, axis=-1))
    weights = jnp.exp(scores - peak[:, None])
    rescale = jnp.exp(private_peak - peak)
    weight_sum = private_sum * rescale + jnp.sum(weights, axis=-1)
    value_sum = private_values * rescale[:, None] + jnp.dot(
        weights.astype(jnp.bfloat16), key_rows[:, :VAL], preferred_element_type=jnp.float32
    )
    attended = (value_sum / weight_sum[:, None]).astype(jnp.bfloat16)
    return attended.reshape(row_count, 2, HEADS * VAL)


def experts(packed, late, hidden, route_ids, route_weights, w_gate, w_up, w_down):
    cache_size = lax.axis_size("cache")
    token_count, width = hidden.shape
    top_count = route_ids.shape[1]
    local_experts = w_gate.shape[0]
    start = lax.axis_index("cache") * token_count
    ids = lax.dynamic_slice_in_dim(route_ids, start, token_count, 0)
    scale = lax.dynamic_slice_in_dim(route_weights, start, token_count, 0)
    high = lax.reduce_precision(scale, 8, 7)
    low = lax.reduce_precision(scale - high, 8, 7)
    routing = jnp.concatenate(
        [
            ids.astype(jnp.bfloat16),
            high.astype(jnp.bfloat16),
            low.astype(jnp.bfloat16),
            jnp.zeros((token_count, EXTRA - 3 * top_count), jnp.bfloat16),
        ],
        axis=1,
    )
    own = jnp.concatenate([hidden, routing], axis=1)
    own, packed = after_all(own, packed)
    gathered = lax.all_gather(packed, "cache", axis=0, tiled=False)
    block = pack([own] + [move_z(own, step, cache_size) for step in range(1, cache_size)])
    first = (lax.axis_index("rep") * local_experts).astype(jnp.int32).reshape(1)

    def work(pieces, plus=()):
        return run_experts(pieces, plus, first, w_gate, w_up, w_down, top_count)

    piece = pack([block, move(block, 1, 1), move(block, 1, -1), move(block, 1, 2)])
    before, after = move(piece, 2, 1), move(piece, 2, -1)
    own_there, own_here = work([[swap_core(piece)], [piece]])
    own_back = swap_core(own_there)
    before, after, own_here, own_there = after_all(before, after, own_here, own_there)
    low, high = halves(before, after)
    low, high = move(low, 2, 1), move(high, 2, -1)
    side_there = work([[swap_core(before)], [swap_core(after)]])
    low, high, *side_there = after_all(low, high, *side_there)
    side_back = [swap_core(part) for part in side_there]
    across_other = [swap_core(low), swap_core(high)]
    (across_here,) = work([[low, high]])
    *across_other, across_here = after_all(*across_other, across_here)
    (across_there,) = work([across_other])
    across_back = swap_core(across_there)
    before, after, across_there = after_all(before, after, across_there)
    sum_before, sum_after = work([[before], [after]], side_back)
    from_after, from_before = move(sum_before, 2, -1), move(sum_after, 2, 1)
    across_back, sum_before, sum_after = after_all(across_back, sum_before, sum_after)
    (sum_across,) = sum_split([across_here, across_back], 1)
    *late, sum_across = after_all(*late, sum_across)
    from_across = move(sum_across, 2, 2)
    line = sum_split([own_here, own_back, from_after, from_before, from_across], SIDE)
    parts = sum_split(
        [line[0], move(line[1], 1, -1), move(line[2], 1, 1), move(line[3], 1, 2)], cache_size
    )
    arrived = [move_z(parts[step], -step, cache_size) for step in range(1, cache_size)]
    return gathered, late, sum_split([parts[0]] + arrived, 1)[0]


def per_device(
    queries,
    pool,
    prefix_pages,
    private_cache,
    private_lengths,
    hidden,
    route_ids,
    route_weights,
    w_gate,
    w_up,
    w_down,
):
    packed, places = held_pages(pool, prefix_pages)
    late = (queries, private_cache, private_lengths, *places)
    gathered, late, mixed = experts(
        packed, late, hidden, route_ids, route_weights, w_gate, w_up, w_down
    )
    queries, private_cache, private_lengths, *places = late
    private = private_attention(queries, private_cache, private_lengths)
    attended = finish_attention(private, gathered, tuple(places), queries.shape[0])
    return (attended, mixed)


def solution(mesh):
    in_specs = (
        P(("rep", "cache"), None, None),
        P("cache", None),
        P("rep", None),
        P(("rep", "cache"), None),
        P(("rep", "cache"), None),
        P(("rep", "cache"), None),
        P("rep", None),
        P("rep", None),
        P("rep", None, "cache"),
        P("rep", None, "cache"),
        P("rep", "cache", None),
    )
    out_specs = (P(("rep", "cache"), None, None), P(("rep", "cache"), None))
    return jax.shard_map(
        per_device, mesh=mesh, in_specs=in_specs, out_specs=out_specs, check_vma=False
    )
```
